32 devices in a mesh: row: 2 (over core), col: 4 (over y, x), cfg: 4 (over z).
Axes of the slice: x: 2, y: 2, z: 4, core: 2. Of those that a mesh axis runs over, the one named last changes fastest.
Arguments:
- eigvec: bfloat16 [18432, 18432], P('row', ('col', 'cfg')), may hold values from -0.046875 to 0.046875
- force_const: bfloat16 [18432, 18432], P(('col', 'cfg'), 'row'), may hold values from -0.046875 to 0.046875
- amplitudes: bfloat16 [18432, 512], P(('col', 'cfg')), may hold values from -6 to 6
- mlip_forces: bfloat16 [18432, 512], P(('col', 'cfg'), 'row'), may hold values from -6 to 6
- frequency: float32 [18432], P(('col', 'cfg')), may hold values from 0.25 to 4
Outputs:
- gradient: float32 [18432, 18432], P(('col', 'cfg'), 'row')
The draws below stay inside these ranges and needn't reach their ends.
All inputs are finite; a program needn't handle non-finite values.
Results may differ from the reference program's by a relative error of at most 0.0055.
Values may be sent and summed in bfloat16 or wider, within the bound.
No kernel may reach another device: no remote copies, remote signals or barrier semaphores. Data moves between devices by JAX's collectives and lax.ppermute only.
A program may use at most 192 MiB of HBM per device.

```python
import math
import jax
import jax.numpy as jnp

NMODES = 18432
CONFIGS = 512


def strengthened(values, own_key, source, target, parts, factor):
    owner, partner = [(jnp.arange(values.shape[position]) // (values.shape[position] // parts)).reshape([-1 if axis == position else 1 for axis in range(values.ndim)]) for position in (source, target)]
    chosen = jax.random.permutation(own_key, parts)[partner]
    strong = (owner == chosen) | (owner == (partner + parts // 2) % parts)
    return jnp.where(strong, factor * values, values)


def levels(stream_key, shape, shards, low, top_value):
    factor_of = 1.0
    for dim, shards_of in shards:
        steps = jax.random.uniform(jax.random.fold_in(jax.random.fold_in(stream_key, 6), dim), (shards_of,), jnp.float32, low / len(shards), top_value / len(shards))
        factor_of = factor_of * jnp.repeat(jnp.exp(steps), shape[dim] // shards_of).reshape((-1,) + (1,) * (len(shape) - 1 - dim))
    return factor_of


def bell_draw(rng, dims, width, reach, shards=(), kind=jnp.bfloat16):
    entries = width * jax.random.normal(rng, dims, jnp.float32)
    if shards:
        entries = entries * levels(rng, dims, shards, -0.22, 0.18)
    return jnp.clip(entries, -reach, reach).astype(kind)


def noise_with(stream_key, extent, spread, bound, pieces, heavy, kind=jnp.bfloat16):
    result = spread * jax.random.normal(stream_key, extent, jnp.float32)
    if pieces:
        result = result * levels(stream_key, extent, pieces, -0.22, 0.18)
    return jnp.clip(strengthened(result, jax.random.fold_in(stream_key, 3), *heavy), -bound, bound).astype(kind)


def setup_inputs(seed: int = 0) -> dict:
    splits = jax.random.split(jax.random.key(seed), 6)
    eigvec = bell_draw(splits[0], (NMODES, NMODES), NMODES ** -0.5, 0.046875, ((0, 2), (1, 16)))
    force_const = bell_draw(splits[1], (NMODES, NMODES), NMODES ** -0.5, 0.046875, ((0, 16), (1, 2)))
    amplitudes = noise_with(splits[2], (NMODES, CONFIGS), 1.0, 6.0, ((0, 16),), (0, 1, 16, 2.0))
    mlip_forces = bell_draw(splits[3], (NMODES, CONFIGS), 1.0, 6.0, ((0, 16), (1, 2)))
    frequency = jnp.clip(jnp.exp(math.log(4.0) - 2.7725887 * jax.random.uniform(splits[4], (NMODES,), jnp.float32) ** levels(splits[4], (NMODES,), ((0, 16),), -0.2, 0.2)), 0.25, 4.0)
    return {"eigvec": eigvec, "force_const": force_const, "amplitudes": amplitudes, "mlip_forces": mlip_forces, "frequency": frequency}


def reference(eigvec, force_const, amplitudes, mlip_forces, frequency):
    mode_scale = 1.0 / jnp.sqrt(2.0 * frequency)
    scaled_amp = (mode_scale[:, None] * amplitudes.astype(jnp.float32)).astype(jnp.bfloat16)
    displaced = jnp.dot(eigvec, scaled_amp, preferred_element_type=jnp.float32).astype(jnp.bfloat16)
    harmonic = jnp.dot(force_const, displaced, preferred_element_type=jnp.float32)
    residual = (mlip_forces.astype(jnp.float32) + harmonic).astype(jnp.bfloat16)
    total = jnp.dot(residual, displaced.T, preferred_element_type=jnp.float32)
    return total / jnp.sqrt(jnp.float32(CONFIGS))
```

```python
import jax
import jax.numpy as jnp
from jax import lax
from jax.experimental import pallas as pl
from jax.experimental.pallas import tpu as pltpu
from jax.sharding import PartitionSpec as P

BF = jnp.bfloat16
F32 = jnp.float32
MESH = ("row", "col", "cfg")
VMEM = 44 * 1024 * 1024
PARTS = (("apbq", 7), ("abpq", 7), ("abpq", 6), ("pabq", 8), ("apbq", 8))
ORDER = (
    (1, 3, 0, 4, 2, 1, 0, 3, 1, 4, 0, 1, 2, 0, 3, 2, 4, 3, 1, 4,)
    + (0, 2, 0, 3, 1, 3, 4, 1, 2, 4, 0, 3, 2, 1, 4, 2, 0, 4, 3, 2,)
)


def bits_of(size):
    assert size & (size - 1) == 0
    return size.bit_length() - 1


class Grid:
    def __init__(self, sizes):
        self.sizes = sizes
        self.at = tuple(lax.axis_index(name) for name in MESH)
        self.flip = self.at[0] & 1

    def order(self, kind):
        levels = []
        for letter in kind:
            axis = 1 if letter in "ab" else 2
            first = 0 if letter in "ap" else 1
            stop = first + 1 if first == 0 else bits_of(self.sizes[axis])
            levels += [(axis, bit) for bit in range(first, stop)]
        return levels

    def mask(self, level, flip):
        axis, bit = level
        if axis == 2:
            return 0, 1 << bit
        bits = bits_of(self.sizes[1])
        return (1 << (bits - 1 - bit) if flip else 1 << bit), 0

    def mine(self, level):
        axis, bit = level
        if axis == 2:
            return (self.at[2] >> bit) & 1
        bits = bits_of(self.sizes[1])
        return (self.at[1] >> jnp.where(self.flip == 1, bits - 1 - bit, bit)) & 1

    def swap(self, value, level):
        nrow, ncol, ncfg = self.sizes
        pairs = []
        for r in range(nrow):
            dc, dz = self.mask(level, r & 1)
            for c in range(ncol):
                for z in range(ncfg):
                    pairs.append(
                        ((r * ncol + c) * ncfg + z, (r * ncol + (c ^ dc)) * ncfg + (z ^ dz))
                    )
        return lax.ppermute(value, MESH, pairs)


def rows_of(value, start, size):
    return lax.dynamic_slice_in_dim(value, start, size, 0)


def ordered(flag, mine, other, axis=0):
    return jnp.where(
        flag == 0,
        jnp.concatenate([mine, other], axis),
        jnp.concatenate([other, mine], axis),
    )


def tiles_of(size, most):
    count = -(-size // most)
    while size % (16 * count):
        count += 1
    return count, size // count


def params():
    return pltpu.CompilerParams(vmem_limit_bytes=VMEM)


def cost(flops, moved):
    return pl.CostEstimate(flops=flops, bytes_accessed=moved, transcendentals=0)


def piece_kernel(eigvec, amp, row, size, terms, keep):
    count, tile = tiles_of(size, 512)
    depth, configs = amp.shape

    def kernel(at, e, a, *refs):
        value = jnp.dot(e[...], a[...], preferred_element_type=F32)
        for index, term in enumerate(refs[: len(terms)]):
            first = pl.multiple_of(at[index + 1] + pl.program_id(0) * tile, 16)
            value = value + term[pl.ds(first, tile), :].astype(F32)
        refs[len(terms)][...] = value.astype(BF)
        if keep:
            refs[len(terms) + 1][...] = value

    out = pl.BlockSpec((tile, configs), lambda i, at: (i, 0))
    spec = pltpu.PrefetchScalarGridSpec(
        num_scalar_prefetch=1,
        grid=(count,),
        in_specs=[
            pl.BlockSpec(
                (pl.Element(tile), pl.Element(depth)),
                lambda i, at: (pl.multiple_of(at[0] + i * tile, 16), 0),
            ),
            pl.BlockSpec((depth, configs), lambda i, at: (0, 0)),
        ]
        + [pl.BlockSpec(term.shape, lambda i, at: (0, 0)) for term, _ in terms],
        out_specs=[out, out] if keep else [out],
    )
    shapes = [jax.ShapeDtypeStruct((size, configs), BF)]
    if keep:
        shapes.append(jax.ShapeDtypeStruct((size, configs), F32))
    at = jnp.stack([jnp.asarray(v, jnp.int32) for v in [row] + [o for _, o in terms]])
    return pl.pallas_call(
        kernel,
        grid_spec=spec,
        out_shape=shapes,
        compiler_params=params(),
        cost_estimate=cost(2 * size * depth * configs, 2 * size * (depth + configs)),
    )(at, eigvec, amp, *[term for term, _ in terms])


def finish_kernel(force_const, harmonic, displaced, mine, other, base, flag):
    half, configs = mine.shape
    rows = force_const.shape[0]
    count, tile = tiles_of(rows, 288)
    first = harmonic is None

    def kernel(at, k_mine, k_other, d_mine, d_other, *refs):
        total, block = refs[-2:]
        value = jnp.dot(k_mine[...], d_mine[...], preferred_element_type=F32)
        value += jnp.dot(k_other[...], d_other[...], preferred_element_type=F32)
        total[...] = value if first else refs[0][...] + value

        @pl.when(pl.program_id(0) == 0)
        def _():
            block[pl.ds(pl.multiple_of(at[0] * half, 16), half), :] = d_mine[...]
            block[pl.ds(pl.multiple_of((1 - at[0]) * half, 16), half), :] = d_other[...]

    def column(own):
        def index(i, at):
            side = at[0] if own else 1 - at[0]
            return i * tile, pl.multiple_of(base + side * half, 128)

        return pl.BlockSpec((pl.Element(tile), pl.Element(half)), index)

    sums = pl.BlockSpec((tile, configs), lambda i, at: (i, 0))
    whole = pl.BlockSpec((half, configs), lambda i, at: (0, 0))
    extra_specs = [] if first else [sums, pl.BlockSpec(memory_space=pl.ANY)]
    extra = [] if first else [harmonic, displaced]
    spec = pltpu.PrefetchScalarGridSpec(
        num_scalar_prefetch=1,
        grid=(count,),
        in_specs=[column(True), column(False), whole, whole] + extra_specs,
        out_specs=[
            sums,
            pl.BlockSpec((pl.Element(2 * half), pl.Element(configs)), lambda i, at: (base, 0)),
        ],
    )
    return pl.pallas_call(
        kernel,
        grid_spec=spec,
        out_shape=[
            jax.ShapeDtypeStruct((rows, configs), F32),
            jax.ShapeDtypeStruct((force_const.shape[1], configs), BF),
        ],
        input_output_aliases={} if first else {5: 0, 6: 1},
        compiler_params=params(),
        cost_estimate=cost(4 * rows * half * configs, 4 * rows * half),
    )(jnp.asarray(flag, jnp.int32)[None], force_const, force_const, mine, other, *extra)


def gradient_kernel(forces, harmonic, got, displaced):
    rows, configs = harmonic.shape
    columns = displaced.shape[0]
    tile = 512
    scale = float(1.0 / configs**0.5)

    def kernel(f, h, g, d, out, residual):
        @pl.when(pl.program_id(0) == 0)
        def _():
            total = f[...].astype(F32) + (h[...] + g[...].astype(F32))
            residual[...] = total.astype(BF)

        value = lax.dot_general(
            residual[...], d[...], (((1,), (1,)), ((), ())), preferred_element_type=F32
        )
        out[...] = value * scale

    whole = pl.BlockSpec((rows, configs), lambda i: (0, 0))
    return pl.pallas_call(
        kernel,
        grid=(columns // tile,),
        in_specs=[whole, whole, whole, pl.BlockSpec((tile, configs), lambda i: (i, 0))],
        out_specs=pl.BlockSpec((rows, tile), lambda i: (0, i)),
        out_shape=jax.ShapeDtypeStruct((rows, columns), F32),
        scratch_shapes=[pltpu.VMEM((rows, configs), BF)],
        compiler_params=params(),
        cost_estimate=cost(2 * rows * columns * configs, 4 * rows * columns),
    )(forces, harmonic, got, displaced)


def part_steps(g, piece, kind, base, rows, finish):
    row, size, terms = base, rows, []
    levels = g.order(kind)
    pin = yield None
    for level in levels[:-1]:
        size //= 2
        mine = g.mine(level)
        away = (1 - mine) * size
        sent = piece(pin, row + away, size, [(t, o + away) for t, o in terms], False)[0]
        got = g.swap(sent, level)
        pin = yield sent
        terms = [(t, o + mine * size) for t, o in terms] + [(got, 0)]
        row = row + mine * size
    sent, own = piece(pin, row, size, terms, True)
    got = g.swap(sent, levels[-1])
    pin = yield sent
    block = (pin(own) + got.astype(F32)).astype(BF)
    for level in reversed(levels[1:-1]):
        other = g.swap(block, level)
        pin = yield block
        block = ordered(g.mine(level), pin(block), other)
    other = g.swap(block, levels[0])
    pin = yield block
    yield finish(base, pin(block), other, g.mine(levels[0]))


def local(sizes, eigvec, force_const, amplitudes, mlip_forces, frequency):
    g = Grid(sizes)
    rows = eigvec.shape[0]
    tiled = rows % (36 * 2 * 16 * sizes[1] * sizes[2] // 2) == 0
    mode_scale = 1.0 / jnp.sqrt(2.0 * frequency)
    scaled_amp = (mode_scale[:, None] * amplitudes.astype(F32)).astype(BF)
    configs = scaled_amp.shape[1]

    def piece(pin, row, size, terms, keep):
        if tiled:
            return piece_kernel(eigvec, pin(scaled_amp), row, size, terms, keep)
        value = jnp.dot(rows_of(eigvec, row, size), pin(scaled_amp), preferred_element_type=F32)
        for term, offset in terms:
            value = value + rows_of(term, offset, size).astype(F32)
        return value.astype(BF), value

    forces = mlip_forces
    for bit in range(bits_of(sizes[0])):
        pairs = [(r, r ^ (1 << bit)) for r in range(sizes[0])]
        forces = ordered((g.at[0] >> bit) & 1, forces, lax.ppermute(forces, "row", pairs), 1)
    state = {"harmonic": None, "displaced": None}

    def finish(base, mine, other, flag):
        harmonic, displaced = state["harmonic"], state["displaced"]
        if tiled:
            harmonic, displaced = finish_kernel(
                force_const, harmonic, displaced, mine, other, base, flag
            )
        else:
            block = ordered(flag, mine, other)
            count = block.shape[0]
            if harmonic is None:
                harmonic = jnp.zeros((force_const.shape[0], configs), F32)
                displaced = jnp.zeros((rows, configs), BF)
            harmonic = harmonic + jnp.dot(
                force_const[:, base : base + count], block, preferred_element_type=F32
            )
            displaced = lax.dynamic_update_slice_in_dim(displaced, block, base, 0)
        state["harmonic"], state["displaced"] = harmonic, displaced
        return harmonic

    steps, base = [], 0
    for kind, units in PARTS:
        count = rows * units // 36
        steps.append(part_steps(g, piece, kind, base, count, finish))
        next(steps[-1])
        base += count
    assert base == rows
    last = [None]

    def pin(value):
        if last[0] is None:
            return value
        return lax.optimization_barrier((value, last[0]))[0]

    for index in schedule(len(PARTS), 2 * len(g.order(PARTS[0][0]))):
        last[0] = steps[index].send(pin)
    harmonic, displaced = state["harmonic"], state["displaced"]
    for bit in range(bits_of(sizes[0])):
        pairs = [(r, r ^ (1 << bit)) for r in range(sizes[0])]
        got = lax.ppermute(harmonic.astype(BF), "row", pairs)
        if not tiled or bit + 1 < bits_of(sizes[0]):
            harmonic = harmonic + got.astype(F32)
    if tiled:
        return gradient_kernel(forces, harmonic, got, displaced)
    residual = (forces.astype(F32) + harmonic).astype(BF)
    out = lax.dot_general(
        residual, displaced, (((1,), (1,)), ((), ())), preferred_element_type=F32
    )
    return out / jnp.sqrt(F32(configs))


def schedule(parts, steps):
    if len(ORDER) == parts * steps:
        return ORDER
    return [part for _ in range(steps) for part in range(parts)]


def solution(mesh):
    sizes = tuple(mesh.shape[name] for name in MESH)

    def body(*args):
        return local(sizes, *args)

    return jax.shard_map(
        body,
        mesh=mesh,
        in_specs=(
            P("row", ("col", "cfg")),
            P(("col", "cfg"), "row"),
            P(("col", "cfg"), None),
            P(("col", "cfg"), "row"),
            P(("col", "cfg")),
        ),
        out_specs=P(("col", "cfg"), "row"),
        check_vma=False,
    )
```

```python
import jax
import jax.numpy as jnp
from jax import lax
from jax.experimental import pallas as pl
from jax.experimental.pallas import tpu as pltpu
from jax.sharding import PartitionSpec as P

BF = jnp.bfloat16
F32 = jnp.float32
MESH = ("row", "col", "cfg")
PARTS = (("abpq", 7), ("apbq", 8), ("abpq", 6), ("pabq", 8), ("apbq", 7))
ORDER = (
    (0, 3, 1, 4, 2, 0, 1, 3, 0, 4, 1, 0, 2, 1, 3, 2, 4, 3, 0, 4,)
    + (1, 2, 1, 0, 3, 0, 4, 3, 2, 4, 1, 0, 2, 3, 4, 2, 1, 4, 3, 2,)
)


def bits_of(size):
    assert size & (size - 1) == 0
    return size.bit_length() - 1


class Grid:
    def __init__(self, sizes):
        self.sizes = sizes
        self.at = tuple(lax.axis_index(name) for name in MESH)
        self.flip = self.at[0] & 1

    def order(self, kind):
        levels = []
        for letter in kind:
            axis = 1 if letter in "ab" else 2
            first = 0 if letter in "ap" else 1
            stop = first + 1 if first == 0 else bits_of(self.sizes[axis])
            levels += [(axis, bit) for bit in range(first, stop)]
        return levels

    def mask(self, level, flip):
        axis, bit = level
        if axis == 2:
            return 0, 1 << bit
        bits = bits_of(self.sizes[1])
        return (1 << (bits - 1 - bit) if flip else 1 << bit), 0

    def mine(self, level):
        axis, bit = level
        if axis == 2:
            return (self.at[2] >> bit) & 1
        bits = bits_of(self.sizes[1])
        return (self.at[1] >> jnp.where(self.flip == 1, bits - 1 - bit, bit)) & 1

    def swap(self, value, level):
        nrow, ncol, ncfg = self.sizes
        pairs = []
        for r in range(nrow):
            dc, dz = self.mask(level, r & 1)
            for c in range(ncol):
                for z in range(ncfg):
                    pairs.append(
                        ((r * ncol + c) * ncfg + z, (r * ncol + (c ^ dc)) * ncfg + (z ^ dz))
                    )
        return lax.ppermute(value, MESH, pairs)


def rows_of(value, start, size):
    return lax.dynamic_slice_in_dim(value, start, size, 0)


def ordered(flag, mine, other, axis=0):
    return jnp.where(
        flag == 0,
        jnp.concatenate([mine, other], axis),
        jnp.concatenate([other, mine], axis),
    )


def tiles_of(size, most, whole):
    count = -(-size // most)
    length = -(-size // (count * whole)) * whole
    return [(at, min(length, size - at)) for at in range(0, size, length)]


def params(mib):
    return pltpu.CompilerParams(vmem_limit_bytes=mib * 1024 * 1024)


def cost(flops, moved):
    return pl.CostEstimate(flops=flops, bytes_accessed=moved, transcendentals=0)


def scalars(values):
    return jnp.stack([jnp.asarray(value, jnp.int32) for value in values])


IN_SMEM = pl.BlockSpec(memory_space=pltpu.SMEM)
IN_VMEM = pl.BlockSpec(memory_space=pltpu.VMEM)
ANYWHERE = pl.BlockSpec(memory_space=pl.ANY)


def finish_kernel(force_const, harmonic, mine, other, base, flag, final):
    half, configs = mine.shape
    rows = force_const.shape[0]
    first = harmonic is None
    chunks = tiles_of(half, 512, 128)
    loads = [(side, start, length) for side in (0, 1) for start, length in chunks]

    def kernel(at, k, d_mine, d_other, *refs):
        total, (held, block, sem, d_sem) = refs[1 - first], refs[-4:]
        copies, blocks = [], []
        for side, source in enumerate((d_mine, d_other)):
            blocks.append(pltpu.make_async_copy(source, block.at[side], d_sem.at[side]))
        for index, (side, start, length) in enumerate(loads):
            which = at[0] if side == 0 else 1 - at[0]
            column = pl.multiple_of(base + which * half + start, 128)
            copies.append(
                pltpu.make_async_copy(
                    k.at[:, pl.ds(column, length)],
                    held.at[:, pl.ds(side * half + start, length)],
                    sem.at[index],
                )
            )
        for copy in [blocks[0], copies[0], blocks[1]] + copies[1:]:
            copy.start()
        for index, (side, start, length) in enumerate(loads):
            if start == 0:
                blocks[side].wait()
            copies[index].wait()
            value = jnp.dot(
                held[:, pl.ds(side * half + start, length)],
                block[side, pl.ds(start, length), :],
                preferred_element_type=F32,
            )
            if index > 0:
                value = value + total[...]
            elif not first:
                value = value + refs[0][...]
            total[...] = value
            if final and index + 1 == len(loads):
                refs[-5][...] = value.astype(BF)

    shapes = [jax.ShapeDtypeStruct((rows, configs), F32)]
    if final:
        shapes.append(jax.ShapeDtypeStruct((rows, configs), BF))
    return pl.pallas_call(
        kernel,
        in_specs=[IN_SMEM, ANYWHERE, ANYWHERE, ANYWHERE] + ([] if first else [IN_VMEM]),
        out_specs=[IN_VMEM] * len(shapes),
        out_shape=shapes,
        scratch_shapes=[
            pltpu.VMEM((rows, 2 * half), BF),
            pltpu.VMEM((2, half, configs), BF),
            pltpu.SemaphoreType.DMA((len(loads),)),
            pltpu.SemaphoreType.DMA((2,)),
        ],
        input_output_aliases={} if first else {4: 0},
        compiler_params=params(44),
        cost_estimate=cost(4 * rows * half * configs, 4 * rows * half),
    )(scalars([flag]), force_const, mine, other, *([] if first else [harmonic]))


def gradient_kernel(side, own_forces, other_forces, harmonic, got, blocks):
    rows, configs = harmonic.shape
    width = own_forces.shape[1]
    scale = float(1.0 / configs**0.5)
    columns = sum(2 * block[2].shape[0] for block in blocks)
    halves, tiles = [], []
    for index, (base, _, mine, other) in enumerate(blocks):
        for part, value in enumerate((mine, other)):
            for start, length in tiles_of(value.shape[0], 512, 128):
                tiles.append((index, part, len(halves), base, value.shape[0], start, length))
            halves.append(value)
    widest = max(tile[-1] for tile in tiles)
    slots = 4

    def kernel(at, f_own, f_other, h, g, *refs):
        sources, out = refs[: len(halves)], refs[len(halves)]
        residual, made, sem, loaded = refs[len(halves) + 1 : len(halves) + 5]
        held = refs[len(halves) + 5 :]
        loads = [
            pltpu.make_async_copy(source, target, loaded.at[index])
            for index, (source, target) in enumerate(zip(sources, held))
        ]
        for load in loads:
            load.start()
        for part, forces in ((0, f_own), (1, f_other)):
            which = at[0] if part == 0 else 1 - at[0]
            lanes = pl.ds(pl.multiple_of(which * width, 128), width)
            total = forces[...].astype(F32) + (h[:, lanes] + g[:, lanes].astype(F32))
            residual[:, lanes] = total.astype(BF)
        copies = []
        for number, (index, part, half, base, size, start, length) in enumerate(tiles):
            slot = number % slots
            if number >= slots:
                copies[number - slots].wait()
            if start == 0:
                loads[half].wait()
            value = lax.dot_general(
                residual[...],
                held[half][pl.ds(start, length), :],
                (((1,), (1,)), ((), ())),
                preferred_element_type=F32,
            )
            made[slot, :, pl.ds(0, length)] = value * scale
            which = at[index + 1] if part == 0 else 1 - at[index + 1]
            column = pl.multiple_of(base + which * size + start, 128)
            copies.append(
                pltpu.make_async_copy(
                    made.at[slot, :, pl.ds(0, length)],
                    out.at[:, pl.ds(column, length)],
                    sem.at[slot],
                )
            )
            copies[-1].start()
        for copy in copies[-slots:]:
            copy.wait()

    return pl.pallas_call(
        kernel,
        in_specs=[IN_SMEM] + [IN_VMEM] * 4 + [ANYWHERE] * len(halves),
        out_specs=ANYWHERE,
        out_shape=jax.ShapeDtypeStruct((rows, columns), F32),
        scratch_shapes=[
            pltpu.VMEM((rows, configs), BF),
            pltpu.VMEM((slots, rows, widest), F32),
            pltpu.SemaphoreType.DMA((slots,)),
            pltpu.SemaphoreType.DMA((len(halves),)),
        ]
        + [pltpu.VMEM(half.shape, BF) for half in halves],
        compiler_params=params(58),
        cost_estimate=cost(2 * rows * columns * configs, 4 * rows * columns),
    )(
        scalars([side] + [block[1] for block in blocks]),
        own_forces,
        other_forces,
        harmonic,
        got,
        *halves,
    )


def part_steps(g, piece, kind, base, rows, finish):
    row, size, terms = base, rows, []
    levels = g.order(kind)
    pin = yield None
    for level in levels[:-1]:
        size //= 2
        mine = g.mine(level)
        away = (1 - mine) * size
        sent = piece(pin, row + away, size, [(t, o + away) for t, o in terms]).astype(BF)
        got = g.swap(sent, level)
        pin = yield sent
        terms = [(t, o + mine * size) for t, o in terms] + [(got, 0)]
        row = row + mine * size
    own = piece(pin, row, size, terms)
    sent = own.astype(BF)
    got = g.swap(sent, levels[-1])
    pin = yield sent
    block = (pin(own) + got.astype(F32)).astype(BF)
    for level in reversed(levels[1:-1]):
        other = g.swap(block, level)
        pin = yield block
        block = ordered(g.mine(level), pin(block), other)
    other = g.swap(block, levels[0])
    pin = yield block
    yield finish(base, pin(block), other, g.mine(levels[0]))


def local(sizes, eigvec, force_const, amplitudes, mlip_forces, frequency):
    g = Grid(sizes)
    rows = eigvec.shape[0]
    tiled = sizes[0] == 2 and rows % (36 * 256) == 0 and sizes[1] * sizes[2] == 16
    mode_scale = 1.0 / jnp.sqrt(2.0 * frequency)
    scaled_amp = (mode_scale[:, None] * amplitudes.astype(F32)).astype(BF)
    configs = scaled_amp.shape[1]

    def piece(pin, row, size, terms):
        value = jnp.dot(rows_of(eigvec, row, size), pin(scaled_amp), preferred_element_type=F32)
        for term, offset in terms:
            value = value + rows_of(term, offset, size).astype(F32)
        return value

    def row_swap(value, bit):
        pairs = [(r, r ^ (1 << bit)) for r in range(sizes[0])]
        return lax.ppermute(value, "row", pairs)

    state = {"harmonic": None, "displaced": jnp.zeros((rows, configs), BF)}
    blocks = []

    def finish(base, mine, other, flag):
        if tiled:
            blocks.append((base, flag, mine, other))
            final = len(blocks) == len(PARTS)
            sums = finish_kernel(
                force_const, state["harmonic"], mine, other, base, flag, final
            )
            state["harmonic"] = sums[0]
            return sums[-1]
        block = ordered(flag, mine, other)
        term = jnp.dot(
            force_const[:, base : base + block.shape[0]], block, preferred_element_type=F32
        )
        state["harmonic"] = term if state["harmonic"] is None else state["harmonic"] + term
        state["displaced"] = lax.dynamic_update_slice_in_dim(state["displaced"], block, base, 0)
        return state["harmonic"]

    steps, base = [], 0
    for kind, units in PARTS:
        count = rows * units // 36
        steps.append(part_steps(g, piece, kind, base, count, finish))
        next(steps[-1])
        base += count
    assert base == rows
    last = [None]

    def pin(value):
        if last[0] is None:
            return value
        return lax.optimization_barrier((value, last[0]))[0]

    for number, index in enumerate(schedule(len(PARTS), 2 * len(g.order(PARTS[0][0])))):
        last[0] = steps[index].send(pin)
        if tiled and number == len(PARTS):
            other_forces = row_swap(pin(mlip_forces), 0)
        if tiled and number == 3 * len(PARTS):
            last[0] = (last[0], other_forces)
    harmonic = state["harmonic"]
    if tiled:
        got = row_swap(last[0], 0)
        return gradient_kernel(g.at[0], mlip_forces, other_forces, harmonic, got, blocks)
    forces = mlip_forces
    for bit in range(bits_of(sizes[0])):
        forces = ordered((g.at[0] >> bit) & 1, forces, row_swap(forces, bit), 1)
    for bit in range(bits_of(sizes[0])):
        harmonic = harmonic + row_swap(harmonic.astype(BF), bit).astype(F32)
    residual = (forces.astype(F32) + harmonic).astype(BF)
    out = lax.dot_general(
        residual, state["displaced"], (((1,), (1,)), ((), ())), preferred_element_type=F32
    )
    return out / jnp.sqrt(F32(configs))


def schedule(parts, steps):
    if len(ORDER) == parts * steps:
        return ORDER
    return [part for _ in range(steps) for part in range(parts)]


def solution(mesh):
    sizes = tuple(mesh.shape[name] for name in MESH)

    def body(*args):
        return local(sizes, *args)

    return jax.shard_map(
        body,
        mesh=mesh,
        in_specs=(
            P("row", ("col", "cfg")),
            P(("col", "cfg"), "row"),
            P(("col", "cfg"), None),
            P(("col", "cfg"), "row"),
            P(("col", "cfg")),
        ),
        out_specs=P(("col", "cfg"), "row"),
        check_vma=False,
    )
```

```python
import jax
import jax.numpy as jnp
from jax import lax
from jax.experimental import pallas as pl
from jax.experimental.pallas import tpu as pltpu
from jax.sharding import PartitionSpec as P

BF = jnp.bfloat16
F32 = jnp.float32
MESH = ("row", "col", "cfg")
PARTS = (("apbq", 7), ("pabq", 8), ("apbq", 7), ("abpq", 7), ("abpq", 7))
ORDER = (
    (3, 1, 2, 0, 4, 3, 2, 1, 3, 0, 2, 3, 4, 2, 1, 0, 4, 1, 0, 3,)
    + (2, 4, 2, 1, 3, 1, 0, 3, 4, 0, 1, 2, 4, 3, 0, 4, 2, 0, 1, 4,)
)


def bits_of(size):
    assert size & (size - 1) == 0
    return size.bit_length() - 1


class Grid:
    def __init__(self, sizes):
        self.sizes = sizes
        self.at = tuple(lax.axis_index(name) for name in MESH)
        self.flip = self.at[0] & 1

    def order(self, kind):
        levels = []
        for letter in kind:
            axis = 1 if letter in "ab" else 2
            first = 0 if letter in "ap" else 1
            stop = first + 1 if first == 0 else bits_of(self.sizes[axis])
            levels += [(axis, bit) for bit in range(first, stop)]
        return levels

    def mask(self, level, flip):
        axis, bit = level
        if axis == 2:
            return 0, 1 << bit
        bits = bits_of(self.sizes[1])
        return (1 << (bits - 1 - bit) if flip else 1 << bit), 0

    def mine(self, level):
        axis, bit = level
        if axis == 2:
            return (self.at[2] >> bit) & 1
        bits = bits_of(self.sizes[1])
        return (self.at[1] >> jnp.where(self.flip == 1, bits - 1 - bit, bit)) & 1

    def swap(self, value, level):
        nrow, ncol, ncfg = self.sizes
        pairs = []
        for r in range(nrow):
            dc, dz = self.mask(level, r & 1)
            for c in range(ncol):
                for z in range(ncfg):
                    pairs.append(
                        ((r * ncol + c) * ncfg + z, (r * ncol + (c ^ dc)) * ncfg + (z ^ dz))
                    )
        return lax.ppermute(value, MESH, pairs)


def rows_of(value, start, size):
    return lax.dynamic_slice_in_dim(value, start, size, 0)


def ordered(flag, mine, other, axis=0):
    return jnp.where(
        flag == 0,
        jnp.concatenate([mine, other], axis),
        jnp.concatenate([other, mine], axis),
    )


def tiles_of(size, most, whole):
    count = -(-size // most)
    length = -(-size // (count * whole)) * whole
    return [(at, min(length, size - at)) for at in range(0, size, length)]


def params(mib):
    return pltpu.CompilerParams(vmem_limit_bytes=mib * 1024 * 1024)


def cost(flops, moved):
    return pl.CostEstimate(flops=flops, bytes_accessed=moved, transcendentals=0)


def scalars(values):
    return jnp.stack([jnp.asarray(value, jnp.int32) for value in values])


IN_SMEM = pl.BlockSpec(memory_space=pltpu.SMEM)
IN_VMEM = pl.BlockSpec(memory_space=pltpu.VMEM)
ANYWHERE = pl.BlockSpec(memory_space=pl.ANY)


def finish_kernel(force_const, harmonic, mine, other, base, flag, final):
    half, configs = mine.shape
    rows = force_const.shape[0]
    first = harmonic is None
    chunks = tiles_of(half, 512, 128)
    loads = [(side, start, length) for side in (0, 1) for start, length in chunks]

    def kernel(at, k, d_mine, d_other, *refs):
        total, (held, block, sem, d_sem) = refs[1 - first], refs[-4:]
        copies, blocks = [], []
        for side, source in enumerate((d_mine, d_other)):
            blocks.append(pltpu.make_async_copy(source, block.at[side], d_sem.at[side]))
        for index, (side, start, length) in enumerate(loads):
            which = at[0] if side == 0 else 1 - at[0]
            column = pl.multiple_of(base + which * half + start, 128)
            copies.append(
                pltpu.make_async_copy(
                    k.at[:, pl.ds(column, length)],
                    held.at[:, pl.ds(side * half + start, length)],
                    sem.at[index],
                )
            )
        for copy in [blocks[0], copies[0], blocks[1]] + copies[1:]:
            copy.start()
        for index, (side, start, length) in enumerate(loads):
            if start == 0:
                blocks[side].wait()
            copies[index].wait()
            value = jnp.dot(
                held[:, pl.ds(side * half + start, length)],
                block[side, pl.ds(start, length), :],
                preferred_element_type=F32,
            )
            if index > 0:
                value = value + total[...]
            elif not first:
                value = value + refs[0][...]
            total[...] = value
            if final and index + 1 == len(loads):
                refs[-5][...] = value.astype(BF)

    shapes = [jax.ShapeDtypeStruct((rows, configs), F32)]
    if final:
        shapes.append(jax.ShapeDtypeStruct((rows, configs), BF))
    return pl.pallas_call(
        kernel,
        in_specs=[IN_SMEM, ANYWHERE, ANYWHERE, ANYWHERE] + ([] if first else [IN_VMEM]),
        out_specs=[IN_VMEM] * len(shapes),
        out_shape=shapes,
        scratch_shapes=[
            pltpu.VMEM((rows, 2 * half), BF),
            pltpu.VMEM((2, half, configs), BF),
            pltpu.SemaphoreType.DMA((len(loads),)),
            pltpu.SemaphoreType.DMA((2,)),
        ],
        input_output_aliases={} if first else {4: 0},
        compiler_params=params(44),
        cost_estimate=cost(1, 1),
    )(scalars([flag]), force_const, mine, other, *([] if first else [harmonic]))


def gradient_kernel(side, own_forces, other_forces, harmonic, got, blocks):
    rows, configs = harmonic.shape
    width = own_forces.shape[1]
    scale = float(1.0 / configs**0.5)
    columns = sum(2 * block[2].shape[0] for block in blocks)
    halves, tiles = [], []
    for index, (base, _, mine, other) in enumerate(blocks):
        for part, value in enumerate((mine, other)):
            for start, length in tiles_of(value.shape[0], 1024, 128):
                tiles.append((index, part, len(halves), base, value.shape[0], start, length))
            halves.append(value)
    widest = max(tile[-1] for tile in tiles)
    slots = 3

    def kernel(at, f_own, f_other, h, g, *refs):
        sources, out = refs[: len(halves)], refs[len(halves)]
        residual, made, sem, loaded = refs[len(halves) + 1 : len(halves) + 5]
        held = refs[len(halves) + 5 :]
        loads = [
            pltpu.make_async_copy(source, target, loaded.at[index])
            for index, (source, target) in enumerate(zip(sources, held))
        ]
        for load in loads:
            load.start()
        for part, forces in ((0, f_own), (1, f_other)):
            which = at[0] if part == 0 else 1 - at[0]
            lanes = pl.ds(pl.multiple_of(which * width, 128), width)
            total = forces[...].astype(F32) + (h[:, lanes] + g[:, lanes].astype(F32))
            residual[:, lanes] = total.astype(BF)
        copies = []
        for number, (index, part, half, base, size, start, length) in enumerate(tiles):
            slot = number % slots
            if number >= slots:
                copies[number - slots].wait()
            if start == 0:
                loads[half].wait()
            value = lax.dot_general(
                residual[...],
                held[half][pl.ds(start, length), :],
                (((1,), (1,)), ((), ())),
                preferred_element_type=F32,
            )
            made[slot, :, pl.ds(0, length)] = value * scale
            which = at[index + 1] if part == 0 else 1 - at[index + 1]
            column = pl.multiple_of(base + which * size + start, 128)
            copies.append(
                pltpu.make_async_copy(
                    made.at[slot, :, pl.ds(0, length)],
                    out.at[:, pl.ds(column, length)],
                    sem.at[slot],
                )
            )
            copies[-1].start()
        for copy in copies[-slots:]:
            copy.wait()

    return pl.pallas_call(
        kernel,
        in_specs=[IN_SMEM] + [IN_VMEM] * 4 + [ANYWHERE] * len(halves),
        out_specs=ANYWHERE,
        out_shape=jax.ShapeDtypeStruct((rows, columns), F32),
        scratch_shapes=[
            pltpu.VMEM((rows, configs), BF),
            pltpu.VMEM((slots, rows, widest), F32),
            pltpu.SemaphoreType.DMA((slots,)),
            pltpu.SemaphoreType.DMA((len(halves),)),
        ]
        + [pltpu.VMEM(half.shape, BF) for half in halves],
        compiler_params=params(58),
        cost_estimate=cost(2 * rows * columns * configs, 4 * rows * columns),
    )(
        scalars([side] + [block[1] for block in blocks]),
        own_forces,
        other_forces,
        harmonic,
        got,
        *halves,
    )


def part_steps(g, piece, kind, base, rows, finish):
    row, size, terms = base, rows, []
    levels = g.order(kind)
    pin = yield None
    for level in levels[:-1]:
        size //= 2
        mine = g.mine(level)
        away = (1 - mine) * size
        sent = piece(pin, row + away, size, [(t, o + away) for t, o in terms]).astype(BF)
        got = g.swap(sent, level)
        pin = yield sent
        terms = [(t, o + mine * size) for t, o in terms] + [(got, 0)]
        row = row + mine * size
    own = piece(pin, row, size, terms)
    sent = own.astype(BF)
    got = g.swap(sent, levels[-1])
    pin = yield sent
    block = (pin(own) + got.astype(F32)).astype(BF)
    for level in reversed(levels[1:-1]):
        other = g.swap(block, level)
        pin = yield block
        block = ordered(g.mine(level), pin(block), other)
    other = g.swap(block, levels[0])
    pin = yield block
    yield finish(base, pin(block), other, g.mine(levels[0]))


def local(sizes, eigvec, force_const, amplitudes, mlip_forces, frequency):
    g = Grid(sizes)
    rows = eigvec.shape[0]
    tiled = sizes[0] == 2 and rows % (36 * 256) == 0 and sizes[1] * sizes[2] == 16
    mode_scale = 1.0 / jnp.sqrt(2.0 * frequency)
    scaled_amp = (mode_scale[:, None] * amplitudes.astype(F32)).astype(BF)
    configs = scaled_amp.shape[1]

    def piece(pin, row, size, terms):
        value = jnp.dot(rows_of(eigvec, row, size), pin(scaled_amp), preferred_element_type=F32)
        for term, offset in terms:
            value = value + rows_of(term, offset, size).astype(F32)
        return value

    def row_swap(value, bit):
        pairs = [(r, r ^ (1 << bit)) for r in range(sizes[0])]
        return lax.ppermute(value, "row", pairs)

    state = {"harmonic": None, "displaced": jnp.zeros((rows, configs), BF)}
    blocks = []

    def finish(base, mine, other, flag):
        if tiled:
            blocks.append((base, flag, mine, other))
            final = len(blocks) == len(PARTS)
            sums = finish_kernel(
                force_const, state["harmonic"], mine, other, base, flag, final
            )
            state["harmonic"] = sums[0]
            return sums[-1]
        block = ordered(flag, mine, other)
        term = jnp.dot(
            force_const[:, base : base + block.shape[0]], block, preferred_element_type=F32
        )
        state["harmonic"] = term if state["harmonic"] is None else state["harmonic"] + term
        state["displaced"] = lax.dynamic_update_slice_in_dim(state["displaced"], block, base, 0)
        return state["harmonic"]

    steps, base = [], 0
    for kind, units in PARTS:
        count = rows * units // 36
        steps.append(part_steps(g, piece, kind, base, count, finish))
        next(steps[-1])
        base += count
    assert base == rows
    last = [None]

    def pin(value):
        if last[0] is None:
            return value
        return lax.optimization_barrier((value, last[0]))[0]

    for number, index in enumerate(schedule(len(PARTS), 2 * len(g.order(PARTS[0][0])))):
        last[0] = steps[index].send(pin)
        if tiled and number == len(PARTS):
            other_forces = row_swap(pin(mlip_forces), 0)
        if tiled and number == 3 * len(PARTS):
            last[0] = (last[0], other_forces)
    harmonic = state["harmonic"]
    if tiled:
        got = row_swap(last[0], 0)
        return gradient_kernel(g.at[0], mlip_forces, other_forces, harmonic, got, blocks)
    forces = mlip_forces
    for bit in range(bits_of(sizes[0])):
        forces = ordered((g.at[0] >> bit) & 1, forces, row_swap(forces, bit), 1)
    for bit in range(bits_of(sizes[0])):
        harmonic = harmonic + row_swap(harmonic.astype(BF), bit).astype(F32)
    residual = (forces.astype(F32) + harmonic).astype(BF)
    out = lax.dot_general(
        residual, state["displaced"], (((1,), (1,)), ((), ())), preferred_element_type=F32
    )
    return out / jnp.sqrt(F32(configs))


def schedule(parts, steps):
    if len(ORDER) == parts * steps:
        return ORDER
    return [part for _ in range(steps) for part in range(parts)]


def solution(mesh):
    sizes = tuple(mesh.shape[name] for name in MESH)

    def body(*args):
        return local(sizes, *args)

    return jax.shard_map(
        body,
        mesh=mesh,
        in_specs=(
            P("row", ("col", "cfg")),
            P(("col", "cfg"), "row"),
            P(("col", "cfg"), None),
            P(("col", "cfg"), "row"),
            P(("col", "cfg")),
        ),
        out_specs=P(("col", "cfg"), "row"),
        check_vma=False,
    )
```

```python
import jax
import jax.numpy as jnp
from jax import lax
from jax.experimental import pallas as pl
from jax.experimental.pallas import tpu as pltpu
from jax.sharding import PartitionSpec as P

BF = jnp.bfloat16
F32 = jnp.float32
MESH = ("row", "col", "cfg")
PARTS = (("apbq", 7), ("pabq", 8), ("apbq", 7), ("abpq", 7), ("abpq", 7))
ORDER = (
    (3, 1, 2, 0, 4, 3, 2, 1, 3, 0, 2, 3, 4, 2, 1, 0, 4, 1, 0, 3,)
    + (2, 4, 2, 1, 3, 1, 0, 3, 4, 0, 1, 2, 4, 3, 0, 4, 2, 0, 1, 4,)
)


def bits_of(size):
    assert size & (size - 1) == 0
    return size.bit_length() - 1


class Grid:
    def __init__(self, sizes):
        self.sizes = sizes
        self.at = tuple(lax.axis_index(name) for name in MESH)
        self.flip = self.at[0] & 1

    def order(self, kind):
        levels = []
        for letter in kind:
            axis = 1 if letter in "ab" else 2
            first = 0 if letter in "ap" else 1
            stop = first + 1 if first == 0 else bits_of(self.sizes[axis])
            levels += [(axis, bit) for bit in range(first, stop)]
        return levels

    def mask(self, level, flip):
        axis, bit = level
        if axis == 2:
            return 0, 1 << bit
        bits = bits_of(self.sizes[1])
        return (1 << (bits - 1 - bit) if flip else 1 << bit), 0

    def mine(self, level):
        axis, bit = level
        if axis == 2:
            return (self.at[2] >> bit) & 1
        bits = bits_of(self.sizes[1])
        return (self.at[1] >> jnp.where(self.flip == 1, bits - 1 - bit, bit)) & 1

    def swap(self, value, level):
        nrow, ncol, ncfg = self.sizes
        pairs = []
        for r in range(nrow):
            dc, dz = self.mask(level, r & 1)
            for c in range(ncol):
                for z in range(ncfg):
                    pairs.append(
                        ((r * ncol + c) * ncfg + z, (r * ncol + (c ^ dc)) * ncfg + (z ^ dz))
                    )
        return lax.ppermute(value, MESH, pairs)


def rows_of(value, start, size):
    return lax.dynamic_slice_in_dim(value, start, size, 0)


def ordered(flag, mine, other, axis=0):
    return jnp.where(
        flag == 0,
        jnp.concatenate([mine, other], axis),
        jnp.concatenate([other, mine], axis),
    )


def tiles_of(size, most, whole):
    count = -(-size // most)
    length = -(-size // (count * whole)) * whole
    return [(at, min(length, size - at)) for at in range(0, size, length)]


def params(mib):
    return pltpu.CompilerParams(vmem_limit_bytes=mib * 1024 * 1024)


def cost(flops, moved):
    return pl.CostEstimate(flops=flops, bytes_accessed=moved, transcendentals=0)


def scalars(values):
    return jnp.stack([jnp.asarray(value, jnp.int32) for value in values])


IN_SMEM = pl.BlockSpec(memory_space=pltpu.SMEM)
IN_VMEM = pl.BlockSpec(memory_space=pltpu.VMEM)
ANYWHERE = pl.BlockSpec(memory_space=pl.ANY)


def finish_kernel(force_const, harmonic, mine, other, base, flag, final):
    half, configs = mine.shape
    rows = force_const.shape[0]
    first = harmonic is None
    chunks = tiles_of(half, 512, 128)
    loads = [(side, start, length) for side in (0, 1) for start, length in chunks]

    def kernel(at, k, d_mine, d_other, *refs):
        total, (held, block, sem, d_sem) = refs[1 - first], refs[-4:]
        copies, blocks = [], []
        for side, source in enumerate((d_mine, d_other)):
            blocks.append(pltpu.make_async_copy(source, block.at[side], d_sem.at[side]))
        for index, (side, start, length) in enumerate(loads):
            which = at[0] if side == 0 else 1 - at[0]
            column = pl.multiple_of(base + which * half + start, 128)
            copies.append(
                pltpu.make_async_copy(
                    k.at[:, pl.ds(column, length)],
                    held.at[:, pl.ds(side * half + start, length)],
                    sem.at[index],
                )
            )
        for copy in [blocks[0], copies[0], blocks[1]] + copies[1:]:
            copy.start()
        for index, (side, start, length) in enumerate(loads):
            if start == 0:
                blocks[side].wait()
            copies[index].wait()
            value = jnp.dot(
                held[:, pl.ds(side * half + start, length)],
                block[side, pl.ds(start, length), :],
                preferred_element_type=F32,
            )
            if index > 0:
                value = value + total[...]
            elif not first:
                value = value + refs[0][...]
            total[...] = value
            if final and index + 1 == len(loads):
                refs[-5][...] = value.astype(BF)

    shapes = [jax.ShapeDtypeStruct((rows, configs), F32)]
    if final:
        shapes.append(jax.ShapeDtypeStruct((rows, configs), BF))
    return pl.pallas_call(
        kernel,
        in_specs=[IN_SMEM, ANYWHERE, ANYWHERE, ANYWHERE] + ([] if first else [IN_VMEM]),
        out_specs=[IN_VMEM] * len(shapes),
        out_shape=shapes,
        scratch_shapes=[
            pltpu.VMEM((rows, 2 * half), BF),
            pltpu.VMEM((2, half, configs), BF),
            pltpu.SemaphoreType.DMA((len(loads),)),
            pltpu.SemaphoreType.DMA((2,)),
        ],
        input_output_aliases={} if first else {4: 0},
        compiler_params=params(44),
        cost_estimate=cost(1, 1),
    )(scalars([flag]), force_const, mine, other, *([] if first else [harmonic]))


def gradient_kernel(side, own_forces, other_forces, harmonic, got, blocks):
    rows, configs = harmonic.shape
    width = own_forces.shape[1]
    scale = float(1.0 / configs**0.5)
    columns = sum(2 * block[2].shape[0] for block in blocks)
    halves, tiles = [], []
    for index, (base, _, mine, other) in enumerate(blocks):
        for part, value in enumerate((mine, other)):
            for start, length in tiles_of(value.shape[0], 1024, 128):
                tiles.append((index, part, len(halves), base, value.shape[0], start, length))
            halves.append(value)
    widest = max(tile[-1] for tile in tiles)
    slots = 3

    def kernel(at, f_own, f_other, h, g, *refs):
        sources, out = refs[: len(halves)], refs[len(halves)]
        residual, made, sem, loaded, g_held, g_sem = refs[len(halves) + 1 : len(halves) + 7]
        held = refs[len(halves) + 7 :]
        g_load = pltpu.make_async_copy(g, g_held, g_sem)
        g_load.start()
        loads = [
            pltpu.make_async_copy(source, target, loaded.at[index])
            for index, (source, target) in enumerate(zip(sources, held))
        ]
        for load in loads:
            load.start()
        g_load.wait()
        for part, forces in ((0, f_own), (1, f_other)):
            which = at[0] if part == 0 else 1 - at[0]
            lanes = pl.ds(pl.multiple_of(which * width, 128), width)
            total = forces[...].astype(F32) + (h[:, lanes] + g_held[:, lanes].astype(F32))
            residual[:, lanes] = total.astype(BF)
        copies = []
        for number, (index, part, half, base, size, start, length) in enumerate(tiles):
            slot = number % slots
            if number >= slots:
                copies[number - slots].wait()
            if start == 0:
                loads[half].wait()
            value = lax.dot_general(
                residual[...],
                held[half][pl.ds(start, length), :],
                (((1,), (1,)), ((), ())),
                preferred_element_type=F32,
            )
            made[slot, :, pl.ds(0, length)] = value * scale
            which = at[index + 1] if part == 0 else 1 - at[index + 1]
            column = pl.multiple_of(base + which * size + start, 128)
            copies.append(
                pltpu.make_async_copy(
                    made.at[slot, :, pl.ds(0, length)],
                    out.at[:, pl.ds(column, length)],
                    sem.at[slot],
                )
            )
            copies[-1].start()
        for copy in copies[-slots:]:
            copy.wait()

    return pl.pallas_call(
        kernel,
        in_specs=[IN_SMEM] + [IN_VMEM] * 3 + [ANYWHERE] * (1 + len(halves)),
        out_specs=ANYWHERE,
        out_shape=jax.ShapeDtypeStruct((rows, columns), F32),
        scratch_shapes=[
            pltpu.VMEM((rows, configs), BF),
            pltpu.VMEM((slots, rows, widest), F32),
            pltpu.SemaphoreType.DMA((slots,)),
            pltpu.SemaphoreType.DMA((len(halves),)),
            pltpu.VMEM((rows, configs), BF),
            pltpu.SemaphoreType.DMA,
        ]
        + [pltpu.VMEM(half.shape, BF) for half in halves],
        compiler_params=params(58),
        cost_estimate=cost(2 * rows * columns * configs, 4 * rows * columns),
    )(
        scalars([side] + [block[1] for block in blocks]),
        own_forces,
        other_forces,
        harmonic,
        got,
        *halves,
    )


def part_steps(g, piece, kind, base, rows, finish):
    row, size, terms = base, rows, []
    levels = g.order(kind)
    pin = yield None
    for level in levels[:-1]:
        size //= 2
        mine = g.mine(level)
        away = (1 - mine) * size
        sent = piece(pin, row + away, size, [(t, o + away) for t, o in terms]).astype(BF)
        got = g.swap(sent, level)
        pin = yield sent
        terms = [(t, o + mine * size) for t, o in terms] + [(got, 0)]
        row = row + mine * size
    own = piece(pin, row, size, terms)
    sent = own.astype(BF)
    got = g.swap(sent, levels[-1])
    pin = yield sent
    block = (pin(own) + got.astype(F32)).astype(BF)
    for level in reversed(levels[1:-1]):
        other = g.swap(block, level)
        pin = yield block
        block = ordered(g.mine(level), pin(block), other)
    other = g.swap(block, levels[0])
    pin = yield block
    yield finish(base, pin(block), other, g.mine(levels[0]))


def local(sizes, eigvec, force_const, amplitudes, mlip_forces, frequency):
    g = Grid(sizes)
    rows = eigvec.shape[0]
    tiled = sizes[0] == 2 and rows % (36 * 256) == 0 and sizes[1] * sizes[2] == 16
    mode_scale = 1.0 / jnp.sqrt(2.0 * frequency)
    scaled_amp = (mode_scale[:, None] * amplitudes.astype(F32)).astype(BF)
    configs = scaled_amp.shape[1]

    def piece(pin, row, size, terms):
        value = jnp.dot(rows_of(eigvec, row, size), pin(scaled_amp), preferred_element_type=F32)
        for term, offset in terms:
            value = value + rows_of(term, offset, size).astype(F32)
        return value

    def row_swap(value, bit):
        pairs = [(r, r ^ (1 << bit)) for r in range(sizes[0])]
        return lax.ppermute(value, "row", pairs)

    state = {"harmonic": None, "displaced": jnp.zeros((rows, configs), BF)}
    blocks = []

    def finish(base, mine, other, flag):
        if tiled:
            blocks.append((base, flag, mine, other))
            final = len(blocks) == len(PARTS)
            sums = finish_kernel(
                force_const, state["harmonic"], mine, other, base, flag, final
            )
            state["harmonic"] = sums[0]
            return sums[-1]
        block = ordered(flag, mine, other)
        term = jnp.dot(
            force_const[:, base : base + block.shape[0]], block, preferred_element_type=F32
        )
        state["harmonic"] = term if state["harmonic"] is None else state["harmonic"] + term
        state["displaced"] = lax.dynamic_update_slice_in_dim(state["displaced"], block, base, 0)
        return state["harmonic"]

    steps, base = [], 0
    for kind, units in PARTS:
        count = rows * units // 36
        steps.append(part_steps(g, piece, kind, base, count, finish))
        next(steps[-1])
        base += count
    assert base == rows
    last = [None]

    def pin(value):
        if last[0] is None:
            return value
        return lax.optimization_barrier((value, last[0]))[0]

    for number, index in enumerate(schedule(len(PARTS), 2 * len(g.order(PARTS[0][0])))):
        last[0] = steps[index].send(pin)
        if tiled and number == len(PARTS):
            other_forces = row_swap(pin(mlip_forces), 0)
        if tiled and number == 3 * len(PARTS):
            last[0] = (last[0], other_forces)
    harmonic = state["harmonic"]
    if tiled:
        got = row_swap(last[0], 0)
        return gradient_kernel(g.at[0], mlip_forces, other_forces, harmonic, got, blocks)
    forces = mlip_forces
    for bit in range(bits_of(sizes[0])):
        forces = ordered((g.at[0] >> bit) & 1, forces, row_swap(forces, bit), 1)
    for bit in range(bits_of(sizes[0])):
        harmonic = harmonic + row_swap(harmonic.astype(BF), bit).astype(F32)
    residual = (forces.astype(F32) + harmonic).astype(BF)
    out = lax.dot_general(
        residual, state["displaced"], (((1,), (1,)), ((), ())), preferred_element_type=F32
    )
    return out / jnp.sqrt(F32(configs))


def schedule(parts, steps):
    if len(ORDER) == parts * steps:
        return ORDER
    return [part for _ in range(steps) for part in range(parts)]


def solution(mesh):
    sizes = tuple(mesh.shape[name] for name in MESH)

    def body(*args):
        return local(sizes, *args)

    return jax.shard_map(
        body,
        mesh=mesh,
        in_specs=(
            P("row", ("col", "cfg")),
            P(("col", "cfg"), "row"),
            P(("col", "cfg"), None),
            P(("col", "cfg"), "row"),
            P(("col", "cfg")),
        ),
        out_specs=P(("col", "cfg"), "row"),
        check_vma=False,
    )
```
